32 devices in a mesh: tracer: 2 (over core), dev: 16 (over z, y, x).
Axes of the slice: x: 2, y: 2, z: 4, core: 2. Of those that a mesh axis runs over, the one named last changes fastest.
Arguments:
- coeffs: bfloat16 [2, 256, 32, 2047], P('tracer', 'dev'), may hold values from -6 to 6
- bessel: bfloat16 [2, 1536, 512, 256], P('tracer', 'dev'), may hold values from -0.375 to 0.375
- azimuthal_order_slots: int32 [16], replicated, may hold values from 0 to 1440, as said below
Outputs:
- cross: float32 [2, 768, 512, 512], P('tracer', 'dev')
The draws below stay inside these ranges and needn't reach their ends.
Inputs may be any that keep to these rules, and one draw needn't show every extreme that they name: `azimuthal_order_slots`: the 16 values are exactly the multiples k * (96) for k = 0 .. 15, each once, in an order drawn from the seed.
All inputs are finite; a program needn't handle non-finite values.
Results may differ from the reference program's by a relative error of at most 0.008.
Values may be sent and summed in bfloat16 or wider, within the bound.
A program may use at most 128 MiB of HBM per device.

```python
import jax
import jax.numpy as jnp
from jax import lax

NSIDE = 512
CYCLES = 2047
LMAX = 1536
SHELLS = 256
KMODES = 512
LB = 128
MWIN = 16
DEGREES_DEV = 96
HALF_DEV = 48


def draw_azimuthal_order_slots(key, part):
    stride = LMAX // MWIN
    shuffled = jax.random.permutation(key, jnp.arange(MWIN, dtype=jnp.int32))
    return (shuffled * stride).astype(jnp.int32)


def levels(key, shape, cuts, smallest, top_value):
    level = 1.0
    for axis_at, blocks in cuts:
        steps = jax.random.uniform(jax.random.fold_in(jax.random.fold_in(key, 6), axis_at), (blocks,), jnp.float32, smallest / len(cuts), top_value / len(cuts))
        level = level * jnp.repeat(jnp.exp(steps), shape[axis_at] // blocks).reshape((-1,) + (1,) * (len(shape) - 1 - axis_at))
    return level


def scatter_about(own_key, extent, deviation, reach, split=(), kind=jnp.bfloat16):
    entries = jax.random.normal(own_key, extent, jnp.float32) * deviation
    if len(split) > 0:
        entries = levels(own_key, extent, split, -0.22, 0.18) * entries
    return jnp.clip(entries, min=-reach, max=reach).astype(kind)


def setup_inputs(seed: int = 0) -> dict:
    key_of = jax.random.split(jax.random.key(seed), 4)
    coeffs = scatter_about(key_of[0], (2, SHELLS, 2 * MWIN, CYCLES), 1.0, 6.0, ((0, 2), (1, 16)))
    bessel = scatter_about(key_of[1], (2, LMAX, KMODES, SHELLS), SHELLS ** -0.5, 0.375, ((0, 2), (1, 16)))
    azimuthal_order_slots = draw_azimuthal_order_slots(jax.random.fold_in(key_of[3], 71), 0)
    return dict(coeffs=coeffs, bessel=bessel, azimuthal_order_slots=azimuthal_order_slots)


rescale_limit = 10000000000.0

def cycle_geometry():
    cycle_number = jnp.arange(1, CYCLES + 1, dtype=jnp.float32)
    nside_float = jnp.float32(NSIDE)
    folded = jnp.minimum(cycle_number, 4.0 * nside_float - cycle_number)
    polar_cycle = folded < nside_float
    polar_gap = folded * folded / (3.0 * nside_float * nside_float)
    equator_height = 4.0 / 3.0 - 2.0 * folded / (3.0 * nside_float)
    cycle_height = jnp.where(polar_cycle, 1.0 - polar_gap, equator_height)
    height_gap = jnp.where(polar_cycle, polar_gap, 1.0 - equator_height)
    sine_cycle = jnp.sqrt(height_gap * (1.0 + cycle_height))
    cosine_latitude = jnp.where(cycle_number <= 2.0 * nside_float, cycle_height, -cycle_height)
    pixels = jnp.where(polar_cycle, 4.0 * folded, 4.0 * nside_float)
    weight = jnp.sqrt(jnp.pi * pixels / (3.0 * nside_float * nside_float))
    return (cosine_latitude, sine_cycle, weight)

def legendre_seed(orders, sine_cycle):
    counter = jnp.arange(1, LMAX + 1, dtype=jnp.float32)
    log_terms = jnp.log1p(-0.5 / counter)
    partial_sum = lax.optimization_barrier(jnp.sum(jnp.where(counter[None, :] <= orders[:, None], log_terms[None, :], 0.0), axis=1))
    head = 0.5 * jnp.log((2.0 * orders + 1.0) / (4.0 * jnp.pi)) + 0.5 * partial_sum
    return head[:, None] + orders[:, None] * jnp.log(sine_cycle)[None, :]

def recurrence_step(carried, degree, orders, cosine_latitude, seed_log):
    previous, current, log_scale = carried
    order_col = orders[:, None]
    alpha_coef = jnp.sqrt(jnp.maximum(4.0 * degree * degree - 1.0, 1.0) / jnp.maximum(degree * degree - order_col * order_col, 1.0))
    degree_below = degree - 1.0
    beta_coef = jnp.sqrt(jnp.maximum(degree_below * degree_below - order_col * order_col, 0.0) / jnp.maximum(4.0 * degree_below * degree_below - 1.0, 1.0))
    starting_degree = degree == order_col
    updated = jnp.where(starting_degree, 1.0, alpha_coef * (cosine_latitude[None, :] * current - beta_coef * previous))
    previous = jnp.where(starting_degree, 0.0, current)
    log_scale = jnp.where(starting_degree, seed_log, log_scale)
    table_value = jnp.where(degree >= order_col, updated * jnp.exp(log_scale), 0.0)
    largest = jnp.maximum(jnp.abs(updated), jnp.abs(previous))
    oversized = largest > rescale_limit
    factor = jnp.where(oversized, 1.0 / jnp.maximum(largest, 1.0), 1.0)
    log_scale = log_scale + jnp.where(oversized, jnp.log(jnp.maximum(largest, 1.0)), 0.0)
    return ((previous * factor, updated * factor, log_scale), table_value)

def legendre_block(carried, first_degree, orders, cosine_latitude, seed_log, weight):

    def advance(inner_state, offset):
        degree = (first_degree + offset).astype(jnp.float32)
        return recurrence_step(inner_state, degree, orders, cosine_latitude, seed_log)
    carried, values = lax.scan(advance, carried, jnp.arange(LB, dtype=jnp.int32), unroll=8)
    return (carried, (values * weight[None, None, :]).astype(jnp.bfloat16))

def reference(coeffs, bessel, azimuthal_order_slots):
    cosine_latitude, sine_cycle, weight = cycle_geometry()
    orders = azimuthal_order_slots.astype(jnp.float32)
    seed_log = legendre_seed(orders, sine_cycle)
    window = azimuthal_order_slots.shape[0]
    grouped_coefficients = coeffs.reshape(2, SHELLS, window, 2, CYCLES).astype(jnp.float32)
    zero_rows = jnp.zeros((window, CYCLES), jnp.float32)
    initial = (zero_rows, zero_rows, zero_rows)

    def one_block(carried, block_index):
        carried, weighted_harmonics = legendre_block(carried, block_index * LB, orders, cosine_latitude, seed_log, weight)
        block_terms = jnp.einsum('lkr,tskcr->tkcls', weighted_harmonics.astype(jnp.float32), grouped_coefficients).astype(jnp.bfloat16)
        return (carried, block_terms)
    final_state, blocks = lax.scan(one_block, initial, jnp.arange(LMAX // LB, dtype=jnp.int32))
    harmonic = jnp.transpose(blocks, (1, 0, 4, 2, 3, 5)).reshape(2, LMAX, 2 * window, SHELLS)
    position = jnp.arange(LMAX, dtype=jnp.int32)
    half_index = position // (LMAX // 2)
    within = position % (LMAX // 2)
    degree_list = within // HALF_DEV * DEGREES_DEV + half_index * HALF_DEV + within % HALF_DEV

    def one_degree(degree):
        leading = jnp.dot(harmonic[0, degree], bessel[0, degree].T, preferred_element_type=jnp.float32).astype(jnp.bfloat16)
        trailing = jnp.dot(harmonic[1, degree], bessel[1, degree].T, preferred_element_type=jnp.float32).astype(jnp.bfloat16)
        tally = jnp.sum((azimuthal_order_slots <= degree).astype(jnp.int32))
        factor = 1.0 / jnp.sqrt(2.0 * tally.astype(jnp.float32))
        return jnp.dot(leading.T, trailing, preferred_element_type=jnp.float32) * factor
    cross = lax.map(one_degree, degree_list)
    return cross.reshape(2, LMAX // 2, KMODES, KMODES)
```

```python
import functools

import jax
import jax.numpy as jnp
from jax import lax
from jax.experimental import pallas as pl
from jax.experimental.pallas import tpu as pltpu
from jax.sharding import PartitionSpec as P

RESCALE_LIMIT = 1e10
LANES = 128
GROUP = 2


def north_geometry(nside):
    folded = jnp.arange(1, 2 * nside + 1, dtype=jnp.float32)
    nside_float = jnp.float32(nside)
    polar_cycle = folded < nside_float
    polar_gap = folded * folded / (3.0 * nside_float * nside_float)
    equator_height = 4.0 / 3.0 - 2.0 * folded / (3.0 * nside_float)
    cosine = jnp.where(polar_cycle, 1.0 - polar_gap, equator_height)
    height_gap = jnp.where(polar_cycle, polar_gap, 1.0 - equator_height)
    sine = jnp.sqrt(height_gap * (1.0 + cosine))
    pixels = jnp.where(polar_cycle, 4.0 * folded, 4.0 * nside_float)
    weight = jnp.sqrt(jnp.pi * pixels / (3.0 * nside_float * nside_float))
    return cosine, sine, weight


def legendre_seed(orders, sine, lmax):
    counter = jnp.arange(1, lmax + 1, dtype=jnp.float32)
    log_terms = jnp.log1p(-0.5 / counter)
    partial_sum = jnp.sum(
        jnp.where(counter[None, :] <= orders[:, None], log_terms[None, :], 0.0), axis=1
    )
    head = 0.5 * jnp.log((2.0 * orders + 1.0) / (4.0 * jnp.pi)) + 0.5 * partial_sum
    return head[:, None] + orders[:, None] * jnp.log(sine)[None, :]


def recurrence_coefficients(orders, lmax):
    degree = jnp.arange(lmax, dtype=jnp.float32)[None, :]
    order_col = orders[:, None]
    alpha = jnp.sqrt(
        jnp.maximum(4.0 * degree * degree - 1.0, 1.0)
        / jnp.maximum(degree * degree - order_col * order_col, 1.0)
    )
    below = degree - 1.0
    beta = jnp.sqrt(
        jnp.maximum(below * below - order_col * order_col, 0.0)
        / jnp.maximum(4.0 * below * below - 1.0, 1.0)
    )
    starting = degree == order_col
    return jnp.where(starting, 1.0, alpha), jnp.where(starting, 1.0, beta)


def harmonic_kernel(lines, slots, lb, unroll, alpha_ref, beta_ref, cosine_ref, weight_ref,
                    seed_ref, coef_ref, out_ref, prev_ref, cur_ref, log_ref, scale_ref, table):
    block = pl.program_id(0)
    half = lax.axis_index("tracer")
    rows = cosine_ref.shape[0]
    part = coef_ref.shape[1] // 2

    @pl.when(block == 0)
    def _():
        for ref in (prev_ref, cur_ref, log_ref, scale_ref):
            ref[...] = jnp.zeros_like(ref)

    out_ref[...] = jnp.zeros_like(out_ref)
    cosine = cosine_ref[...]
    weight = weight_ref[...]
    active = (block - half + lines) // lines

    def group(g, carry):
        picks = [g * GROUP + i for i in range(GROUP)]
        state = []
        for p in picks:
            starting = p * lines + half == block
            log_scale = jnp.where(starting, seed_ref[p], log_ref[p])
            scale = jnp.where(starting, jnp.exp(log_scale) * weight, scale_ref[p])
            state.append((jnp.where(starting, -1.0, prev_ref[p]), cur_ref[p], log_scale, scale))

        def chunk(c, state):
            state = list(state)
            for u in range(unroll):
                offset = c * unroll + u
                for i, p in enumerate(picks):
                    prev, cur, log_scale, scale = state[i]
                    a = alpha_ref[0, 0, p * lb + offset]
                    b = beta_ref[0, 0, p * lb + offset]
                    new = a * (cosine * cur - b * prev)
                    table[i, pl.ds(pl.multiple_of(offset * rows, rows), rows), :] = new * scale
                    state[i] = (cur, new, log_scale, scale)
            for i in range(GROUP):
                prev, cur, log_scale, scale = state[i]
                largest = jnp.maximum(jnp.abs(prev), jnp.abs(cur))
                oversized = largest > RESCALE_LIMIT
                safe = jnp.maximum(largest, 1.0)
                factor = jnp.where(oversized, 1.0 / safe, 1.0)
                log_scale = log_scale + jnp.where(oversized, jnp.log(safe), 0.0)
                state[i] = (prev * factor, cur * factor, log_scale, jnp.exp(log_scale) * weight)
            return tuple(state)

        state = lax.fori_loop(0, lb // unroll, chunk, tuple(state))
        for i, p in enumerate(picks):
            prev_ref[p], cur_ref[p], log_ref[p], scale_ref[p] = state[i]
            values = jnp.concatenate(
                [table[i, pl.ds(s, lb, stride=rows), :].astype(jnp.bfloat16) for s in range(rows)],
                axis=1,
            )
            both = lax.dot_general(
                coef_ref[p], values, (((1,), (1,)), ((), ())), preferred_element_type=jnp.float32
            )
            offset = lax.broadcasted_iota(jnp.int32, (part, lb), 1)
            odd = (offset + (block + p * lines + half) * lb) % 2 == 1
            chosen = jnp.where(odd, both[part:], both[:part]).astype(jnp.bfloat16)
            each = part // lines
            for t in range(lines):
                out_ref[t, 0, p] = chosen[t * each:(t + 1) * each]
        return carry

    lax.fori_loop(0, (active + GROUP - 1) // GROUP, group, 0)


def harmonic_blocks(alpha, beta, cosine, weight, seed, coefficients, lines):
    blocks, slots, lb = alpha.shape[0], seed.shape[0], alpha.shape[2] // seed.shape[0]
    north = seed.shape[1] * LANES
    each = coefficients.shape[1] // (2 * lines)
    unroll = max(u for u in range(1, 9) if lb % u == 0)
    rows = north // LANES
    whole = lambda x: pl.BlockSpec(x.shape, lambda b: (0,) * x.ndim)
    scalar = pl.BlockSpec((1, 1, slots * lb), lambda b: (b, 0, 0), memory_space=pltpu.SMEM)
    return pl.pallas_call(
        functools.partial(harmonic_kernel, lines, slots, lb, unroll),
        grid=(blocks,),
        out_shape=jax.ShapeDtypeStruct((lines, blocks, slots, each, lb), jnp.bfloat16),
        in_specs=[scalar, scalar, whole(cosine), whole(weight), whole(seed), whole(coefficients)],
        out_specs=pl.BlockSpec((lines, 1, slots, each, lb), lambda b: (0, b, 0, 0, 0)),
        scratch_shapes=[pltpu.VMEM((slots, rows, LANES), jnp.float32)] * 4
        + [pltpu.VMEM((GROUP, lb * rows, LANES), jnp.float32)],
        compiler_params=pltpu.CompilerParams(vmem_limit_bytes=40 * 2**20),
    )(alpha, beta, cosine, weight, seed, coefficients)


def per_device(coeffs, bessel, azimuthal_order_slots):
    lines, devices = lax.axis_size("tracer"), lax.axis_size("dev")
    tracer_id, device = lax.axis_index("tracer"), lax.axis_index("dev")
    _, shells, _, cycles = coeffs.shape
    window = azimuthal_order_slots.shape[0]
    degrees_here = bessel.shape[1]
    lmax = degrees_here * devices
    stride = lmax // window
    nside = (cycles + 1) // 4
    north = 2 * nside
    slots = window // lines

    ranks = jnp.arange(window, dtype=jnp.int32)
    placed = azimuthal_order_slots[None, :] == ranks[:, None] * stride
    placed = jnp.kron(placed.astype(jnp.bfloat16), jnp.eye(2, dtype=jnp.bfloat16))
    rows = jnp.einsum("ij,sjr->isr", placed, coeffs[0], preferred_element_type=jnp.bfloat16)
    rows = rows.reshape(slots, lines, 2 * shells, cycles)
    rows = lax.all_to_all(rows, "tracer", split_axis=1, concat_axis=1, tiled=True)
    rows = rows.reshape(slots, lines * 2 * shells, cycles)
    near = rows[..., :north].astype(jnp.float32)
    far = jnp.pad(rows[..., north:], ((0, 0), (0, 0), (0, 2 * north - cycles)))
    index = jnp.arange(north, dtype=jnp.int32)
    mirror = (index[:, None] + index[None, :] == north - 2).astype(jnp.bfloat16)
    far = jnp.einsum("pnu,uv->pnv", far, mirror, preferred_element_type=jnp.float32)
    coefficients = jnp.concatenate([near + far, near - far], axis=1).astype(jnp.bfloat16)

    cosine, sine, weight = north_geometry(nside)
    orders = ((jnp.arange(slots, dtype=jnp.int32) * lines + tracer_id) * stride).astype(jnp.float32)
    seed = legendre_seed(orders, sine, lmax).reshape(slots, -1, LANES)
    alpha, beta = recurrence_coefficients(orders, lmax)
    by_block = lambda x: x.reshape(slots, window, stride).transpose(1, 0, 2).reshape(window, 1, -1)
    harmonic = harmonic_blocks(
        by_block(alpha), by_block(beta), cosine.reshape(-1, LANES), weight.reshape(-1, LANES),
        seed, coefficients, lines,
    )
    harmonic = harmonic.reshape(lines * devices, slots, 2, shells, stride)
    received = lax.all_to_all(
        harmonic, ("tracer", "dev"), split_axis=0, concat_axis=0, tiled=True
    ).reshape(lines, devices, slots, 2, shells, stride)
    by_degree = received.transpose(5, 0, 2, 3, 1, 4).reshape(stride, 2 * window, devices * shells)

    radial = jnp.einsum(
        "lcs,lks->lck", by_degree, bessel[0], preferred_element_type=jnp.float32
    ).astype(jnp.bfloat16)
    half_depth = degrees_here // 2
    own_half = lax.dynamic_slice_in_dim(radial, tracer_id * half_depth, half_depth, 0)
    outgoing = lax.dynamic_slice_in_dim(radial, (1 - tracer_id) * half_depth, half_depth, 0)
    other_half = lax.ppermute(outgoing, "tracer", [(0, 1), (1, 0)])
    leading = jnp.where(tracer_id == 0, own_half, other_half)
    trailing = jnp.where(tracer_id == 0, other_half, own_half)
    degree_values = (
        device * degrees_here + tracer_id * half_depth + jnp.arange(half_depth, dtype=jnp.int32)
    )
    mode_tallies = jnp.sum(
        (azimuthal_order_slots[None, :] <= degree_values[:, None]).astype(jnp.int32), axis=1
    )
    factor = 1.0 / jnp.sqrt(2.0 * mode_tallies.astype(jnp.float32))
    cross_power_spectrum = (
        jnp.einsum("lck,lcj->lkj", leading, trailing, preferred_element_type=jnp.float32)
        * factor[:, None, None]
    )
    return cross_power_spectrum[None]


def solution(mesh):
    placed = (P("tracer", "dev", None, None), P("tracer", "dev", None, None), P())
    return jax.shard_map(
        per_device,
        mesh=mesh,
        in_specs=placed,
        out_specs=P("tracer", "dev", None, None),
        check_vma=False,
    )
```
